32 devices in a mesh: grp: 4 (over y, core), sub: 8 (over z, x).
Axes of the slice: x: 2, y: 2, z: 4, core: 2. Of those that a mesh axis runs over, the one named last changes fastest.
Arguments:
- right_side: float32 [8192, 2048], P(('grp', 'sub'))
- schur: bfloat16 [16384, 512], P(('grp', 'sub'))
- inv_factor: bfloat16 [16384, 512], P(('grp', 'sub'))
- coarse_inverse: float32 [256, 64], P('grp')
- primal_index: int32 [32, 8], P(('grp', 'sub')), may hold values from 0 to 255
- phase: int32 [8192], P(('grp', 'sub')), may hold values from 0 to 3
- phase_coef: float32 [4], replicated, may hold values from 0.5 to 4
Outputs:
- solution: float32 [8192, 2048], P(('grp', 'sub'))
- residual: float32 [8192, 2048], P(('grp', 'sub'))
The draws below stay inside these ranges and needn't reach their ends.
All inputs are finite; a program needn't handle non-finite values.
Results may differ from the reference program's by a relative error of at most 0.0056.
Values may be sent and summed in bfloat16 or wider, within the bound.
No kernel may reach another device: no remote copies, remote signals or barrier semaphores. Data moves between devices by JAX's collectives and lax.ppermute only.
A program may use at most 64 MiB of HBM per device.

```python
import math
import jax
import jax.numpy as jnp
from jax import lax

NI = 512
NF = 256
NPD = 8
NC = 64
NRHS = 2048
PHASES = 4
SUBS = 32
ROWS = 8192
N_GRP = 4
N_SUB = 8


def draw_right_side(key, part):
    k1, k2, k3 = jax.random.split(key, 3)
    place = jnp.arange(ROWS, dtype=jnp.float32) / ROWS
    row_scale = (0.5 + place) * jnp.exp(jax.random.uniform(k1, (ROWS,), jnp.float32, -1.15, 1.15))
    col_scale = jnp.exp(jax.random.uniform(k2, (NRHS,), jnp.float32, -1.15, 1.15))
    base = jax.random.normal(k3, (ROWS, NRHS), jnp.float32)
    return (row_scale[:, None] * col_scale[None, :] * base).astype(jnp.float32)


def square_eye(width):
    return (jnp.arange(width)[:, None] == jnp.arange(width)[None, :]).astype(jnp.float32)


def draw_schur(key, part):
    k1, k2 = jax.random.split(jax.random.fold_in(key, 11))
    noise = jax.random.normal(k1, (SUBS, NI, NI), jnp.float32)
    sym = 0.6 * (noise + jnp.swapaxes(noise, 1, 2)) / jnp.sqrt(2.0 * NI)
    diag = jax.random.uniform(k2, (SUBS, NI, 1), jnp.float32, 1.5, 3.5)
    return (sym + diag * square_eye(NI)[None]).reshape(SUBS * NI, NI).astype(jnp.bfloat16)


def draw_inv_factor(key, part):
    k1, k2 = jax.random.split(jax.random.fold_in(key, 23))
    noise = 0.5 * jax.random.normal(k1, (SUBS, NI, NI), jnp.float32) / jnp.sqrt(1.0 * NI)
    diag = jax.random.uniform(k2, (SUBS, NI, 1), jnp.float32, 0.8, 1.6)
    return (noise + diag * square_eye(NI)[None]).reshape(SUBS * NI, NI).astype(jnp.bfloat16)


def draw_coarse_inverse(key, part):
    k1, k2, k3 = jax.random.split(jax.random.fold_in(key, 37), 3)
    noise = 0.5 * jax.random.normal(k1, (N_GRP, NC, NC), jnp.float32) / jnp.sqrt(1.0 * NC)
    diag = jax.random.uniform(k2, (N_GRP, NC, 1), jnp.float32, 0.5, 1.0)
    order = jax.random.permutation(k3, N_GRP).astype(jnp.float32)
    level = order / max(N_GRP - 1, 1)
    group_scale = jnp.exp(level * jnp.log(16.0))
    matrix = (noise + diag * square_eye(NC)[None]) * group_scale[:, None, None]
    return matrix.reshape(N_GRP * NC, NC).astype(jnp.float32)


def place_ends(drawn, rng, smallest, high):
    index_at = [jax.random.randint(jax.random.fold_in(rng, axis), (), 0, length) for axis, length in enumerate(drawn.shape)]
    main_axis = drawn.shape.index(max(drawn.shape))
    neighbour = index_at[:main_axis] + [(index_at[main_axis] + 1) % drawn.shape[main_axis]] + index_at[main_axis + 1:]
    return drawn.at[tuple(index_at)].set(smallest).at[tuple(neighbour)].set(high)


def setup_inputs(seed: int = 0) -> dict:
    key_of = jax.random.split(jax.random.key(seed), 8)
    return {
        "right_side": draw_right_side(jax.random.fold_in(key_of[7], 71), 0),
        "schur": draw_schur(jax.random.fold_in(key_of[7], 71), 0),
        "inv_factor": draw_inv_factor(jax.random.fold_in(key_of[7], 71), 0),
        "coarse_inverse": draw_coarse_inverse(jax.random.fold_in(key_of[7], 71), 0),
        "primal_index": place_ends(jax.random.randint(key_of[4], (SUBS, NPD), 0, NF), jax.random.fold_in(key_of[4], 1), 0, NF - 1).astype(jnp.int32),
        "phase": place_ends(jax.random.randint(key_of[5], (ROWS,), 0, PHASES), jax.random.fold_in(key_of[5], 1), 0, PHASES - 1).astype(jnp.int32),
        "phase_coef": jnp.clip(jnp.exp(jax.random.uniform(key_of[6], (PHASES,), jnp.float32, math.log(0.5), math.log(4.0))), 0.5, 4.0),
    }


def extend(block):
    return jnp.concatenate([jnp.roll(block, 1, axis=0), block], axis=1)


def assemble(local):
    return local[:, NF:, :] + jnp.roll(local[:, :NF, :], -1, axis=0)


def reference(right_side, schur, inv_factor, coarse_inverse, primal_index, phase, phase_coef):
    hi = lax.Precision.HIGHEST
    rhs = right_side.reshape(N_GRP, N_SUB, NF, NRHS)
    panels = schur.reshape(N_GRP, N_SUB, NI, NI)
    factors = inv_factor.reshape(N_GRP, N_SUB, NI, NI)
    coarse = coarse_inverse.reshape(N_GRP, NC, NC)
    picks = primal_index.reshape(N_GRP, N_SUB, NPD)
    labels = phase.reshape(N_GRP, N_SUB, NF)
    onehot = (picks[..., None] == jnp.arange(NF, dtype=jnp.int32)).astype(jnp.float32)
    coarse_rhs = jnp.einsum('gskf,gsfr->gskr', onehot, rhs, precision=hi).reshape(N_GRP, NC, NRHS)
    solved = jnp.einsum('gab,gbr->gar', coarse, coarse_rhs, precision=hi)
    shared = jnp.sum(solved, axis=0) / N_GRP
    correction = (solved + shared[None]).reshape(N_GRP, N_SUB, NPD, NRHS)
    table = (jnp.arange(PHASES, dtype=jnp.int32)[None, None, :] == labels[..., None]).astype(jnp.float32)
    coef_rows = jnp.einsum('gsfk,k->gsf', table, phase_coef, precision=hi)

    def one_group(items):
        rhs_g, panel_g, factor_g, onehot_g, corr_g, coef_g = items
        rb = rhs_g.astype(jnp.bfloat16)
        fac = factor_g.astype(jnp.float32)
        first = jnp.einsum('sij,sjr->sir', fac, extend(rb).astype(jnp.float32)).astype(jnp.bfloat16)
        second = jnp.einsum('sji,sjr->sir', fac, first.astype(jnp.float32)).astype(jnp.bfloat16)
        direction = 0.5 * assemble(second.astype(jnp.float32)) + jnp.einsum('skf,skr->sfr', onehot_g, corr_g, precision=hi)
        dirb = direction.astype(jnp.bfloat16)
        rz_group = jnp.sum(rhs_g * direction, axis=(0, 1))
        image = jnp.einsum('sij,sjr->sir', panel_g.astype(jnp.float32), extend(dirb).astype(jnp.float32)).astype(jnp.bfloat16)
        qvec = assemble(image.astype(jnp.float32)) + coef_g[..., None] * dirb.astype(jnp.float32)
        return dirb, qvec, rz_group

    dirb, qvec, rz_parts = lax.map(one_group, (rhs, panels, factors, onehot, correction, coef_rows))
    rz_total = jnp.sum(rz_parts, axis=0)
    pq_total = jnp.sum(dirb.astype(jnp.float32) * qvec, axis=(0, 1, 2))
    alpha = rz_total / pq_total
    solution = (alpha * dirb.astype(jnp.float32)).reshape(ROWS, NRHS)
    residual = (rhs - alpha * qvec).reshape(ROWS, NRHS)
    return solution, residual
```

```python
import functools

import jax
import jax.numpy as jnp
from jax import lax
from jax.experimental import pallas as pl
from jax.experimental.pallas import tpu as pltpu
from jax.sharding import PartitionSpec as P

HIGHEST = lax.Precision.HIGHEST
VMEM = pltpu.VMEM
SMEM = pltpu.SMEM
F32 = jnp.float32
BF16 = jnp.bfloat16


def widths(columns):
    return [columns // 4] * 4


def starts(sizes):
    return [sum(sizes[:i]) for i in range(len(sizes))]


def params():
    return pltpu.CompilerParams(vmem_limit_bytes=40 * 1024 * 1024)


def whole(space=VMEM):
    return pl.BlockSpec(memory_space=space)


def pair_swap(value):
    count = lax.axis_size("sub")
    return lax.ppermute(value, "sub", [(j, j ^ 1) for j in range(count)])


def pass_on(value):
    count = lax.axis_size("sub")
    pairs = [(j, (j + (2 if j % 2 == 0 else -2)) % count) for j in range(count)]
    return lax.ppermute(value, "sub", pairs)


def to_left(value):
    count = lax.axis_size("sub")
    return lax.ppermute(value, "sub", [(j, (j - 1) % count) for j in range(count)])


def summed_over(value, axis):
    count = lax.axis_size(axis)
    if count & (count - 1):
        return lax.psum(value, axis)
    step = 1
    while step < count:
        value = value + lax.ppermute(value, axis, [(i, i ^ step) for i in range(count)])
        step *= 2
    return value


def from_all(value):
    devices = lax.axis_size("grp") * lax.axis_size("sub")
    copies = jnp.broadcast_to(value[None], (devices,) + value.shape)
    return lax.all_to_all(copies, ("grp", "sub"), 0, 0, tiled=True)


def split_kernel(sizes, index_ref, right_ref, primal_ref, *chunk_refs):
    for k in range(primal_ref.shape[0]):
        primal_ref[k : k + 1, :] = right_ref[pl.ds(index_ref[0, k], 1), :]
    for begin, size, chunk_ref in zip(starts(sizes), sizes, chunk_refs):
        chunk_ref[...] = right_ref[:, begin : begin + size].astype(BF16)


def split(right_side, primal_index, sizes):
    rows, columns = right_side.shape
    outs = [jax.ShapeDtypeStruct((primal_index.shape[1], columns), F32)]
    outs += [jax.ShapeDtypeStruct((rows, size), BF16) for size in sizes]
    out = pl.pallas_call(
        functools.partial(split_kernel, sizes),
        out_shape=outs,
        in_specs=[whole(SMEM), whole()],
        out_specs=[whole()] * len(outs),
        compiler_params=params(),
        name="split",
    )(primal_index, right_side)
    return out[0], list(out[1:])


def gram_kernel(factor_ref, upper_ref, lower_ref):
    half = upper_ref.shape[0]
    dims = (((0,), (0,)), ((), ()))
    factor = factor_ref[...]
    product = lax.dot_general(factor, factor, dims, preferred_element_type=F32)
    upper_ref[...] = product[:half].astype(BF16)
    lower_ref[...] = product[half:].astype(BF16)


def gram(factor):
    size = factor.shape[0]
    out = jax.ShapeDtypeStruct((size // 2, size), BF16)
    return pl.pallas_call(
        gram_kernel,
        out_shape=[out, out],
        in_specs=[whole()],
        out_specs=[whole(), whole()],
        compiler_params=params(),
        name="gram",
    )(factor)


def stencil(parity, low, up, swapped, own, passed):
    half = low.shape[0]
    even = parity == 0
    for_swapped = jnp.where(even, up[:, half:], low[:, :half])
    for_passed = jnp.where(even, low[:, :half], up[:, half:])
    dot = functools.partial(jnp.dot, preferred_element_type=F32)
    total = dot(low[:, half:], own) + dot(up[:, :half], own)
    total = total + dot(for_swapped, swapped)
    return total + dot(for_passed, passed)


def direction_kernel(
    parity_ref, index_ref, low_ref, up_ref, swapped_ref, own_ref, passed_ref, right_ref, corr_ref,
    dir_ref, rz_ref, full_ref,
):
    full_ref[...] = 0.5 * stencil(
        parity_ref[0], low_ref[...], up_ref[...], swapped_ref[...], own_ref[...], passed_ref[...]
    )
    for k in range(corr_ref.shape[0]):
        row = pl.ds(index_ref[0, k], 1)
        full_ref[row, :] = full_ref[row, :] + corr_ref[k : k + 1, :]
    full = full_ref[...]
    dir_ref[...] = full.astype(BF16)
    rz_ref[...] = jnp.sum(right_ref[...] * full, axis=0, keepdims=True)


def direction_chunk(parity, index, low, up, swapped, own, passed, right_side, corr, begin):
    rows, size = own.shape
    block = begin // size
    full = lambda a: pl.BlockSpec(a.shape, lambda i: (0,) * a.ndim)
    part = lambda a: pl.BlockSpec((a.shape[0], size), lambda i: (0, block))
    return pl.pallas_call(
        direction_kernel,
        grid=(1,),
        out_shape=[
            jax.ShapeDtypeStruct((rows, size), BF16),
            jax.ShapeDtypeStruct((1, size), F32),
        ],
        in_specs=[whole(SMEM), whole(SMEM)]
        + [full(a) for a in (low, up, swapped, own, passed)]
        + [part(right_side), part(corr)],
        out_specs=[
            pl.BlockSpec((rows, size), lambda i: (0, 0)),
            pl.BlockSpec((1, size), lambda i: (0, 0)),
        ],
        scratch_shapes=[pltpu.VMEM((rows, size), F32)],
        compiler_params=params(),
        name="direction",
    )(parity, index, low, up, swapped, own, passed, right_side, corr)


def image_kernel(
    parity_ref, panel_ref, up_ref, swapped_ref, own_ref, passed_ref, coef_ref, q_ref, pq_ref
):
    own = own_ref[...]
    total = stencil(
        parity_ref[0], panel_ref[...], up_ref[...], swapped_ref[...], own, passed_ref[...]
    )
    own_f = own.astype(F32)
    q = total + coef_ref[:, :1] * own_f
    q_ref[...] = q
    pq_ref[...] = jnp.sum(own_f * q, axis=0, keepdims=True)


def image_chunk(parity, schur, up, swapped, own, passed, coef):
    rows, size = own.shape
    full = lambda a: pl.BlockSpec(a.shape, lambda i: (0,) * a.ndim)
    return pl.pallas_call(
        image_kernel,
        grid=(1,),
        out_shape=[
            jax.ShapeDtypeStruct((rows, size), F32),
            jax.ShapeDtypeStruct((1, size), F32),
        ],
        in_specs=[
            whole(SMEM),
            pl.BlockSpec((rows, 2 * rows), lambda i: (1, 0)),
        ]
        + [full(a) for a in (up, swapped, own, passed, coef)],
        out_specs=[
            pl.BlockSpec((rows, size), lambda i: (0, 0)),
            pl.BlockSpec((1, size), lambda i: (0, 0)),
        ],
        compiler_params=params(),
        name="image",
    )(parity, schur, up, swapped, own, passed, coef)


def update_kernel(sizes, sums_ref, last_ref, right_ref, *refs):
    count = len(sizes)
    dirs, qs, (solution_ref, residual_ref) = refs[:count], refs[count : 2 * count], refs[2 * count :]
    for i, (begin, size) in enumerate(zip(starts(sizes), sizes)):
        if i < count - 1:
            sums = sums_ref[:, begin : begin + size]
        else:
            sums = jnp.sum(last_ref[...], axis=0)
        alpha = sums[0:1] / sums[1:2]
        cols = slice(begin, begin + size)
        solution_ref[:, cols] = alpha * dirs[i][...].astype(F32)
        residual_ref[:, cols] = right_ref[:, cols] - alpha * qs[i][...]


def update(sums, last, right_side, dirs, qs, sizes):
    out = jax.ShapeDtypeStruct(right_side.shape, F32)
    return pl.pallas_call(
        functools.partial(update_kernel, sizes),
        out_shape=[out, out],
        in_specs=[whole()] * (3 + 2 * len(sizes)),
        out_specs=[whole(), whole()],
        compiler_params=params(),
        name="update",
    )(sums, last, right_side, *dirs, *qs)


def body(right_side, schur, inv_factor, coarse_inverse, primal_index, phase, phase_coef):
    face_rows, columns = right_side.shape
    sizes = widths(columns)
    begins = starts(sizes)
    parity = (lax.axis_index("sub") % 2).astype(jnp.int32)[None]

    own_primal, resid = split(right_side, primal_index, sizes)
    swapped = [pair_swap(c) for c in resid]
    gram_up, gram_low = gram(inv_factor)
    gram_next = to_left(gram_up)
    schur_next = to_left(schur[:face_rows])
    passed = [pass_on(c) for c in swapped]

    group_primal = lax.all_to_all(own_primal, "sub", 1, 0, tiled=True)
    solved = jnp.dot(coarse_inverse, group_primal, precision=HIGHEST)
    mean = summed_over(solved, "grp") / lax.axis_size("grp")
    correction = lax.all_to_all(solved + mean, "sub", 0, 1, tiled=True)

    dirs, rzs = [], []
    for i, begin in enumerate(begins):
        d, rz = direction_chunk(
            parity, primal_index, gram_low, gram_next, swapped[i], resid[i], passed[i],
            right_side, correction, begin,
        )
        dirs.append(d)
        rzs.append(rz)
    dir_swapped = [pair_swap(d) for d in dirs]
    dir_passed = [pass_on(d) for d in dir_swapped]

    labels = jnp.arange(phase_coef.shape[0], dtype=jnp.int32)
    coef = jnp.sum(
        jnp.where(phase[:, None] == labels[None, :], phase_coef[None, :], 0.0), axis=1
    )
    coef = jnp.broadcast_to(coef[:, None], (face_rows, 128))

    qs, parts = [], []
    for i in range(len(sizes)):
        q, pq = image_chunk(parity, schur, schur_next, dir_swapped[i], dirs[i], dir_passed[i], coef)
        qs.append(q)
        parts.append(jnp.concatenate([rzs[i], pq], axis=0))
    early = jnp.concatenate(parts[:-1], axis=1)
    early = summed_over(summed_over(early, "grp"), "sub")
    last = from_all(parts[-1])
    return update(early, last, right_side, dirs, qs, sizes)


def solution(mesh):
    in_specs = (
        P(("grp", "sub"), None),
        P(("grp", "sub"), None),
        P(("grp", "sub"), None),
        P("grp", None),
        P(("grp", "sub"), None),
        P(("grp", "sub")),
        P(),
    )
    out_specs = (P(("grp", "sub"), None), P(("grp", "sub"), None))
    return jax.shard_map(body, mesh=mesh, in_specs=in_specs, out_specs=out_specs, check_vma=False)
```

```python
import functools

import jax
import jax.numpy as jnp
from jax import lax
from jax.experimental import pallas as pl
from jax.experimental.pallas import tpu as pltpu
from jax.sharding import PartitionSpec as P

HIGHEST = lax.Precision.HIGHEST
VMEM = pltpu.VMEM
SMEM = pltpu.SMEM
F32 = jnp.float32
BF16 = jnp.bfloat16

EIGHTHS = (2, 2, 2, 2)
TIES = {
    "d0": ("s2",),
    "d3": ("n",),
    "e": ("s0",),
    "g": ("e", "c"),
    "h": ("m", "p1", "s1"),
    "i0": ("x1",),
    "i1": ("x2",),
    "i2": ("x3",),
    "n": ("h",),
    "s1": ("s0",),
    "s2": ("c", "s0"),
    "s3": ("m",),
    "t": ("s1",),
    "u": ("p0",),
    "x0": ("s3",),
    "y0": ("d1",),
}


def widths(columns):
    return [columns // 8 * part for part in EIGHTHS]


def starts(sizes):
    return [sum(sizes[:i]) for i in range(len(sizes))]


def params(mebibytes):
    return pltpu.CompilerParams(vmem_limit_bytes=mebibytes * 1024 * 1024)


def whole(space=VMEM):
    return pl.BlockSpec(memory_space=space)


def shape(rows, columns, dtype):
    return jax.ShapeDtypeStruct((rows, columns), dtype)


def after(value, *others):
    return lax.optimization_barrier((value,) + others)[0]


def exchange(value, axis, step):
    count = lax.axis_size(axis)
    return lax.ppermute(value, axis, [(i, i ^ step) for i in range(count)])


def pair_swap(value):
    return exchange(value, "sub", 1)


def pass_on(value):
    count = lax.axis_size("sub")
    pairs = [(j, (j + (2 if j % 2 == 0 else -2)) % count) for j in range(count)]
    return lax.ppermute(value, "sub", pairs)


def to_left(value):
    count = lax.axis_size("sub")
    return lax.ppermute(value, "sub", [(j, (j - 1) % count) for j in range(count)])


def powers(low, count):
    return [1 << b for b in range(low, count.bit_length() - 1)]


def step_length(rzs, pqs, odd):
    groups, subs = lax.axis_size("grp"), lax.axis_size("sub")
    parts = jnp.concatenate([jnp.concatenate(p, axis=1) for p in (rzs, pqs)], axis=0)
    half = parts.shape[1] // 2
    low, high = parts[:, :half], parts[:, half:]
    mine = jnp.where(odd, high, low) + exchange(jnp.where(odd, low, high), "grp", 1)
    same = [[g * subs + j for g in range(p, groups, 2) for j in range(subs)] for p in range(2)]
    copies = jnp.broadcast_to(mine[None], (len(same[0]),) + mine.shape)
    sums = lax.all_to_all(copies, ("grp", "sub"), 0, 0, axis_index_groups=same, tiled=True)
    alpha = quotient(sums)
    other = exchange(alpha, "grp", 1)
    return jnp.concatenate([jnp.where(odd, other, alpha), jnp.where(odd, alpha, other)], axis=1)


def first_kernel(place_ref, index_ref, right_ref, chunk_ref, primal_ref, face, blocks, sems):
    rank = primal_ref.shape[0]
    size = chunk_ref.shape[1]
    copies = [pltpu.make_async_copy(right_ref.at[:, :size], face, sems.at[rank])]
    for k in range(rank):
        begin = pl.multiple_of((index_ref[0, k] >> 3) << 3, 8)
        source = right_ref.at[pl.ds(begin, 8), :]
        copies.append(pltpu.make_async_copy(source, blocks.at[k], sems.at[k]))
    for copy in copies:
        copy.start()
    copies[0].wait()
    chunk_ref[...] = face[...].astype(BF16)
    for k in range(rank):
        copies[k + 1].wait()
        primal_ref[k : k + 1, :] = blocks[k, pl.ds(index_ref[0, k] & 7, 1), :]


def first_chunk(place, right_side, primal_index, size):
    rows, columns = right_side.shape
    rank = primal_index.shape[1]
    return pl.pallas_call(
        first_kernel,
        out_shape=[shape(rows, size, BF16), shape(rank, columns, F32)],
        in_specs=[whole(SMEM), whole(SMEM), whole(pl.ANY)],
        out_specs=[whole(), whole()],
        scratch_shapes=[
            pltpu.VMEM((rows, size), F32),
            pltpu.VMEM((rank, 8, columns), F32),
            pltpu.SemaphoreType.DMA((rank + 1,)),
        ],
        compiler_params=params(8),
        name="first",
    )(place, primal_index, pltpu.with_memory_space_constraint(right_side, pltpu.HBM))


def split_kernel(sizes, right_ref, after_ref, *chunk_refs):
    for begin, size, chunk_ref in zip(starts(sizes)[1:], sizes[1:], chunk_refs):
        chunk_ref[...] = right_ref[:, begin : begin + size].astype(BF16)


def split(right_side, first, sizes):
    rows = right_side.shape[0]
    outs = [shape(rows, size, BF16) for size in sizes[1:]]
    out = pl.pallas_call(
        functools.partial(split_kernel, sizes),
        out_shape=outs,
        in_specs=[whole(), whole(pl.ANY)],
        out_specs=[whole()] * len(outs),
        compiler_params=params(8),
        name="split",
    )(right_side, first)
    return [first] + list(out)


def gram_kernel(factor_ref, upper_ref, lower_ref):
    half = upper_ref.shape[0]
    dims = (((0,), (0,)), ((), ()))
    factor = factor_ref[...]
    product = lax.dot_general(factor, factor, dims, preferred_element_type=F32)
    upper_ref[...] = product[:half].astype(BF16)
    lower_ref[...] = product[half:].astype(BF16)


def gram(factor):
    size = factor.shape[0]
    out = shape(size // 2, size, BF16)
    return pl.pallas_call(
        gram_kernel,
        out_shape=[out, out],
        in_specs=[whole()],
        out_specs=[whole(), whole()],
        compiler_params=params(8),
        name="gram",
    )(factor)


def solve_kernel(masks, place_ref, matrix_ref, *refs):
    pieces, (own_ref, partner_ref, sorted_ref, rows_ref) = refs[: len(masks)], refs[len(masks) :]
    rank = own_ref.shape[0]
    position = place_ref[2]
    sorted_ref[...] = jnp.zeros_like(sorted_ref)
    for mask, piece in zip(masks, pieces):
        begin = pl.multiple_of((position ^ mask) * rank, rank)
        sorted_ref[pl.ds(begin, rank), :] = piece[...]
    for k, target in enumerate((position, position ^ 1)):
        rows = pl.ds(pl.multiple_of(target * rank, rank), rank)
        rows_ref[k * rank : (k + 1) * rank, :] = matrix_ref[rows, :]
    both = jnp.dot(
        rows_ref[...], sorted_ref[...], precision=HIGHEST, preferred_element_type=F32
    )
    own_ref[...] = both[:rank]
    partner_ref[...] = both[rank:]


def solve(place, matrix, pieces, masks):
    rank, columns = pieces[0].shape
    out = shape(rank, columns, F32)
    return pl.pallas_call(
        functools.partial(solve_kernel, masks),
        out_shape=[out, out],
        in_specs=[whole(SMEM)] + [whole()] * (1 + len(pieces)),
        out_specs=[whole(), whole()],
        scratch_shapes=[
            pltpu.VMEM((matrix.shape[1], columns), F32),
            pltpu.VMEM((2 * rank, matrix.shape[1]), F32),
        ],
        compiler_params=params(8),
        name="solve",
    )(place, matrix, *pieces)


def stencil(parity, low, up, swapped, own, passed):
    half = low.shape[0]
    even = parity == 0
    for_swapped = jnp.where(even, up[:, half:], low[:, :half])
    for_passed = jnp.where(even, low[:, :half], up[:, half:])
    dot = functools.partial(jnp.dot, preferred_element_type=F32)
    total = dot(low[:, half:], own) + dot(up[:, :half], own)
    total = total + dot(for_swapped, swapped)
    return total + dot(for_passed, passed)


def direction_kernel(
    cols, place_ref, index_ref, low_ref, up_ref, swapped_ref, own_ref, passed_ref, right_ref,
    corr_ref, dir_ref, rz_ref, full_ref,
):
    full_ref[...] = 0.5 * stencil(
        place_ref[0], low_ref[...], up_ref[...], swapped_ref[...], own_ref[...], passed_ref[...]
    )
    for k in range(corr_ref.shape[0]):
        row = pl.ds(index_ref[0, k], 1)
        full_ref[row, :] = full_ref[row, :] + corr_ref[k : k + 1, cols]
    full = full_ref[...]
    dir_ref[...] = full.astype(BF16)
    rz_ref[...] = jnp.sum(right_ref[:, cols] * full, axis=0, keepdims=True)


def direction_chunk(place, index, low, up, swapped, own, passed, right_side, corr, begin):
    rows, size = own.shape
    return pl.pallas_call(
        functools.partial(direction_kernel, slice(begin, begin + size)),
        out_shape=[shape(rows, size, BF16), shape(1, size, F32)],
        in_specs=[whole(SMEM)] * 2 + [whole()] * 7,
        out_specs=[whole(), whole()],
        scratch_shapes=[pltpu.VMEM((rows, size), F32)],
        compiler_params=params(12),
        name="direction",
    )(place, index, low, up, swapped, own, passed, right_side, corr)


def image_kernel(
    place_ref, panel_ref, up_ref, swapped_ref, own_ref, passed_ref, coef_ref, q_ref, pq_ref
):
    own = own_ref[...]
    half = own.shape[0]
    total = stencil(
        place_ref[0], panel_ref[half:, :], up_ref[...], swapped_ref[...], own, passed_ref[...]
    )
    own_f = own.astype(F32)
    q = total + coef_ref[:, :1] * own_f
    q_ref[...] = q
    pq_ref[...] = jnp.sum(own_f * q, axis=0, keepdims=True)


def image_chunk(place, schur, up, swapped, own, passed, coef):
    rows, size = own.shape
    return pl.pallas_call(
        image_kernel,
        out_shape=[pltpu.VMEM((rows, size), F32), shape(1, size, F32)],
        in_specs=[whole(SMEM)] + [whole()] * 6,
        out_specs=[whole(), whole()],
        compiler_params=params(12),
        name="image",
    )(place, schur, up, swapped, own, passed, coef)


def quotient_kernel(sums_ref, alpha_ref):
    sums = jnp.sum(sums_ref[...], axis=0)
    alpha_ref[...] = sums[0:1] / sums[1:2]


def quotient(sums):
    return pl.pallas_call(
        quotient_kernel,
        out_shape=shape(1, sums.shape[2], F32),
        in_specs=[whole()],
        out_specs=whole(),
        compiler_params=params(8),
        name="quotient",
    )(sums)


def update_kernel(sizes, alpha_ref, right_ref, *refs):
    count = len(sizes)
    dirs, qs = refs[:count], refs[count : 2 * count]
    solution_ref, residual_ref, solution_buf, residual_buf, sems = refs[2 * count :]
    copies = []
    for i, (begin, size) in enumerate(zip(starts(sizes), sizes)):
        cols = slice(begin, begin + size)
        alpha = alpha_ref[:, cols]
        solution_buf[:, cols] = alpha * dirs[i][...].astype(F32)
        residual_buf[:, cols] = right_ref[:, cols] - alpha * qs[i][...]
        for k, (buf, ref) in enumerate(
            ((solution_buf, solution_ref), (residual_buf, residual_ref))
        ):
            copy = pltpu.make_async_copy(buf.at[:, cols], ref.at[:, cols], sems.at[2 * i + k])
            copy.start()
            copies.append(copy)
    for copy in copies:
        copy.wait()


def update(alpha, right_side, dirs, qs, sizes):
    rows, columns = right_side.shape
    out = shape(rows, columns, F32)
    return pl.pallas_call(
        functools.partial(update_kernel, sizes),
        out_shape=[out, out],
        in_specs=[whole()] * (2 + 2 * len(sizes)),
        out_specs=[whole(pl.ANY)] * 2,
        scratch_shapes=[pltpu.VMEM((rows, columns), F32)] * 2
        + [pltpu.SemaphoreType.DMA((2 * len(sizes),))],
        compiler_params=params(12),
        name="update",
    )(alpha, right_side, *dirs, *qs)


def body(right_side, schur, inv_factor, coarse_inverse, primal_index, phase, phase_coef):
    face_rows, columns = right_side.shape
    sizes = widths(columns)
    begins = starts(sizes)
    chunks = range(len(sizes))
    subs, groups = lax.axis_size("sub"), lax.axis_size("grp")
    rank = primal_index.shape[1]
    position, group = lax.axis_index("sub"), lax.axis_index("grp")
    place = jnp.stack([position % 2, group % 2, position]).astype(jnp.int32)
    place = lax.optimization_barrier(place)

    known = {}

    def get(name):
        if name not in known:
            known[name] = None
            known[name] = made[name[0]](*([int(name[1:])] if name[1:] else []))
        assert known[name] is not None
        return known[name]

    def tied(name, value):
        others = [get(other) for other in TIES.get(name, ())]
        return after(value, *others) if others else value

    primal_index = pltpu.with_memory_space_constraint(primal_index, pltpu.HBM)
    first, own_primal = first_chunk(place, right_side, primal_index, sizes[0])
    resid = split(right_side, first, sizes)

    masks = range(0, subs, 2)
    def gather(i):
        return exchange(tied(f"a{i}", own_primal), "sub", masks[i])

    def solved():
        pieces = [tied("e", own_primal)] + [get(f"a{i}") for i in range(1, len(masks))]
        return solve(place, coarse_inverse, pieces, masks)

    def coarse():
        own, partner = get("e")
        return own + pair_swap(tied("c", partner))

    def total():
        value = tied("t", get("c"))
        for step in powers(0, groups):
            value = value + exchange(value, "grp", step)
            if step == 1:
                value = tied("u", value)
        return get("c") + value / groups

    def direction(i):
        own = tied(f"d{i}", resid[i])
        if i:
            own = after(own, get(f"d{i - 1}")[0])
        return direction_chunk(
            place, primal_index, get("g")[1], get("m"), get(f"s{i}"), own, get(f"p{i}"), right_side,
            get("h"), begins[i],
        )

    def coefficients():
        labels = jnp.arange(phase_coef.shape[0], dtype=jnp.int32)
        coef = jnp.sum(
            jnp.where(phase[:, None] == labels[None, :], phase_coef[None, :], 0.0), axis=1
        )
        return jnp.broadcast_to(coef[:, None], (face_rows, 128))

    def image(i):
        own = tied(f"i{i}", get(f"d{i}")[0])
        if i:
            own = after(own, get(f"i{i - 1}")[1])
        return image_chunk(
            place, schur, get("n"), get(f"x{i}"), own, get(f"y{i}"), get("k")
        )

    made = {
        "a": gather,
        "s": lambda i: pair_swap(tied(f"s{i}", resid[i])),
        "p": lambda i: pass_on(tied(f"p{i}", get(f"s{i}"))),
        "g": lambda: gram(tied("g", inv_factor)),
        "m": lambda: to_left(get("g")[0]),
        "n": lambda: to_left(tied("n", schur)[:face_rows]),
        "e": solved,
        "c": coarse,
        "h": lambda: tied("h", total()),
        "d": direction,
        "x": lambda i: pair_swap(tied(f"x{i}", get(f"d{i}")[0])),
        "y": lambda i: pass_on(tied(f"y{i}", get(f"x{i}"))),
        "k": coefficients,
        "i": image,
    }
    images = [get(f"i{i}") for i in chunks]
    dirs = [get(f"d{i}") for i in chunks]
    alpha = step_length([d[1] for d in dirs], [i[1] for i in images], place[1] == 1)
    return update(alpha, right_side, [d[0] for d in dirs], [i[0] for i in images], sizes)


def solution(mesh):
    in_specs = (
        P(("grp", "sub"), None),
        P(("grp", "sub"), None),
        P(("grp", "sub"), None),
        P("grp", None),
        P(("grp", "sub"), None),
        P(("grp", "sub")),
        P(),
    )
    out_specs = (P(("grp", "sub"), None), P(("grp", "sub"), None))
    return jax.shard_map(body, mesh=mesh, in_specs=in_specs, out_specs=out_specs, check_vma=False)
```

```python
import functools

import jax
import jax.numpy as jnp
from jax import lax
from jax.experimental import pallas as pl
from jax.experimental.pallas import tpu as pltpu
from jax.sharding import PartitionSpec as P

HIGHEST = lax.Precision.HIGHEST
VMEM = pltpu.VMEM
SMEM = pltpu.SMEM
F32 = jnp.float32
BF16 = jnp.bfloat16

EIGHTHS = (2, 2, 2, 2)
TIES = {
    "d0": ("s2",),
    "d3": ("n", "x0"),
    "e": ("s0",),
    "g": ("c", "e"),
    "h": ("m", "s1"),
    "i0": ("x1",),
    "i1": ("x2",),
    "i2": ("x3",),
    "n": ("s2",),
    "s1": ("s0",),
    "s2": ("c", "s0"),
    "s3": ("m",),
    "t": ("s1",),
    "u": ("p0",),
    "x0": ("s3",),
}


def widths(columns):
    return [columns // 8 * part for part in EIGHTHS]


def starts(sizes):
    return [sum(sizes[:i]) for i in range(len(sizes))]


def params(mebibytes):
    return pltpu.CompilerParams(vmem_limit_bytes=mebibytes * 1024 * 1024)


def whole(space=VMEM):
    return pl.BlockSpec(memory_space=space)


def shape(rows, columns, dtype):
    return jax.ShapeDtypeStruct((rows, columns), dtype)


def after(value, *others):
    return lax.optimization_barrier((value,) + others)[0]


def exchange(value, axis, step):
    count = lax.axis_size(axis)
    return lax.ppermute(value, axis, [(i, i ^ step) for i in range(count)])


def pair_swap(value):
    return exchange(value, "sub", 1)


def pass_on(value):
    count = lax.axis_size("sub")
    pairs = [(j, (j + (2 if j % 2 == 0 else -2)) % count) for j in range(count)]
    return lax.ppermute(value, "sub", pairs)


def to_left(value):
    count = lax.axis_size("sub")
    return lax.ppermute(value, "sub", [(j, (j - 1) % count) for j in range(count)])


def powers(low, count):
    return [1 << b for b in range(low, count.bit_length() - 1)]


def step_length(rzs, pqs, odd):
    groups, subs = lax.axis_size("grp"), lax.axis_size("sub")
    parts = jnp.concatenate([jnp.concatenate(p, axis=1) for p in (rzs, pqs)], axis=0)
    half = parts.shape[1] // 2
    low, high = parts[:, :half], parts[:, half:]
    mine = jnp.where(odd, high, low) + exchange(jnp.where(odd, low, high), "grp", 1)
    same = [[g * subs + j for g in range(p, groups, 2) for j in range(subs)] for p in range(2)]
    copies = jnp.broadcast_to(mine[None], (len(same[0]),) + mine.shape)
    sums = lax.all_to_all(copies, ("grp", "sub"), 0, 0, axis_index_groups=same, tiled=True)
    alpha = quotient(sums)
    other = exchange(alpha, "grp", 1)
    return jnp.concatenate([jnp.where(odd, other, alpha), jnp.where(odd, alpha, other)], axis=1)


def first_kernel(place_ref, right_ref, chunk_ref):
    chunk_ref[...] = right_ref[...].astype(BF16)


def first_chunk(place, right_side, size):
    rows = right_side.shape[0]
    block = pl.BlockSpec((rows, size), lambda i: (0, 0))
    return pl.pallas_call(
        first_kernel,
        grid=(1,),
        out_shape=shape(rows, size, BF16),
        in_specs=[whole(SMEM), block],
        out_specs=block,
        compiler_params=params(8),
        name="first",
    )(place, right_side)


def pick_kernel(index_ref, right_ref, after_ref, primal_ref, blocks, sems):
    rank = primal_ref.shape[0]
    copies = []
    for k in range(rank):
        begin = pl.multiple_of((index_ref[0, k] >> 3) << 3, 8)
        source = right_ref.at[pl.ds(begin, 8), :]
        copies.append(pltpu.make_async_copy(source, blocks.at[k], sems.at[k]))
        copies[-1].start()
    for k in range(rank):
        copies[k].wait()
        primal_ref[k : k + 1, :] = blocks[k, pl.ds(index_ref[0, k] & 7, 1), :]


def pick(right_side, primal_index, first):
    columns = right_side.shape[1]
    rank = primal_index.shape[1]
    return pl.pallas_call(
        pick_kernel,
        out_shape=shape(rank, columns, F32),
        in_specs=[whole(SMEM), whole(pl.ANY), whole(pl.ANY)],
        out_specs=whole(),
        scratch_shapes=[
            pltpu.VMEM((rank, 8, columns), F32),
            pltpu.SemaphoreType.DMA((rank,)),
        ],
        compiler_params=params(8),
        name="pick",
    )(primal_index, right_side, first)


def split_kernel(sizes, right_ref, after_ref, *chunk_refs):
    for begin, size, chunk_ref in zip(starts(sizes)[1:], sizes[1:], chunk_refs):
        chunk_ref[...] = right_ref[:, begin : begin + size].astype(BF16)


def split(right_side, first, sizes):
    rows = right_side.shape[0]
    outs = [shape(rows, size, BF16) for size in sizes[1:]]
    out = pl.pallas_call(
        functools.partial(split_kernel, sizes),
        out_shape=outs,
        in_specs=[whole(), whole(pl.ANY)],
        out_specs=[whole()] * len(outs),
        compiler_params=params(8),
        name="split",
    )(right_side, first)
    return [first] + list(out)


def gram_kernel(factor_ref, upper_ref, lower_ref):
    half = upper_ref.shape[0]
    dims = (((0,), (0,)), ((), ()))
    factor = factor_ref[...]
    product = lax.dot_general(factor, factor, dims, preferred_element_type=F32)
    upper_ref[...] = product[:half].astype(BF16)
    lower_ref[...] = product[half:].astype(BF16)


def gram(factor):
    size = factor.shape[0]
    out = shape(size // 2, size, BF16)
    return pl.pallas_call(
        gram_kernel,
        out_shape=[out, out],
        in_specs=[whole()],
        out_specs=[whole(), whole()],
        compiler_params=params(8),
        name="gram",
    )(factor)


def solve_kernel(masks, place_ref, matrix_ref, *refs):
    pieces, (own_ref, partner_ref, sorted_ref, rows_ref) = refs[: len(masks)], refs[len(masks) :]
    rank = own_ref.shape[0]
    position = place_ref[2]
    sorted_ref[...] = jnp.zeros_like(sorted_ref)
    for mask, piece in zip(masks, pieces):
        begin = pl.multiple_of((position ^ mask) * rank, rank)
        sorted_ref[pl.ds(begin, rank), :] = piece[...]
    for k, target in enumerate((position, position ^ 1)):
        rows = pl.ds(pl.multiple_of(target * rank, rank), rank)
        rows_ref[k * rank : (k + 1) * rank, :] = matrix_ref[rows, :]
    both = jnp.dot(
        rows_ref[...], sorted_ref[...], precision=HIGHEST, preferred_element_type=F32
    )
    own_ref[...] = both[:rank]
    partner_ref[...] = both[rank:]


def solve(place, matrix, pieces, masks):
    rank, columns = pieces[0].shape
    out = shape(rank, columns, F32)
    return pl.pallas_call(
        functools.partial(solve_kernel, masks),
        out_shape=[out, out],
        in_specs=[whole(SMEM)] + [whole()] * (1 + len(pieces)),
        out_specs=[whole(), whole()],
        scratch_shapes=[
            pltpu.VMEM((matrix.shape[1], columns), F32),
            pltpu.VMEM((2 * rank, matrix.shape[1]), F32),
        ],
        compiler_params=params(8),
        name="solve",
    )(place, matrix, *pieces)


def stencil(parity, low, up, swapped, own, passed):
    half = low.shape[0]
    even = parity == 0
    for_swapped = jnp.where(even, up[:, half:], low[:, :half])
    for_passed = jnp.where(even, low[:, :half], up[:, half:])
    dot = functools.partial(jnp.dot, preferred_element_type=F32)
    total = dot(low[:, half:], own) + dot(up[:, :half], own)
    total = total + dot(for_swapped, swapped)
    return total + dot(for_passed, passed)


def direction_kernel(
    cols, place_ref, index_ref, low_ref, up_ref, swapped_ref, own_ref, passed_ref, right_ref,
    corr_ref, dir_ref, rz_ref, full_ref,
):
    full_ref[...] = 0.5 * stencil(
        place_ref[0], low_ref[...], up_ref[...], swapped_ref[...], own_ref[...], passed_ref[...]
    )
    for k in range(corr_ref.shape[0]):
        row = pl.ds(index_ref[0, k], 1)
        full_ref[row, :] = full_ref[row, :] + corr_ref[k : k + 1, cols]
    full = full_ref[...]
    dir_ref[...] = full.astype(BF16)
    rz_ref[...] = jnp.sum(right_ref[:, cols] * full, axis=0, keepdims=True)


def direction_chunk(place, index, low, up, swapped, own, passed, right_side, corr, begin):
    rows, size = own.shape
    return pl.pallas_call(
        functools.partial(direction_kernel, slice(begin, begin + size)),
        out_shape=[shape(rows, size, BF16), shape(1, size, F32)],
        in_specs=[whole(SMEM)] * 2 + [whole()] * 7,
        out_specs=[whole(), whole()],
        scratch_shapes=[pltpu.VMEM((rows, size), F32)],
        compiler_params=params(12),
        name="direction",
    )(place, index, low, up, swapped, own, passed, right_side, corr)


def image_kernel(
    place_ref, panel_ref, up_ref, swapped_ref, own_ref, passed_ref, coef_ref, q_ref, pq_ref
):
    own = own_ref[...]
    half = own.shape[0]
    total = stencil(
        place_ref[0], panel_ref[half:, :], up_ref[...], swapped_ref[...], own, passed_ref[...]
    )
    own_f = own.astype(F32)
    q = total + coef_ref[:, :1] * own_f
    q_ref[...] = q
    pq_ref[...] = jnp.sum(own_f * q, axis=0, keepdims=True)


def image_chunk(place, schur, up, swapped, own, passed, coef):
    rows, size = own.shape
    return pl.pallas_call(
        image_kernel,
        out_shape=[pltpu.VMEM((rows, size), F32), shape(1, size, F32)],
        in_specs=[whole(SMEM)] + [whole()] * 6,
        out_specs=[whole(), whole()],
        compiler_params=params(12),
        name="image",
    )(place, schur, up, swapped, own, passed, coef)


def quotient_kernel(sums_ref, alpha_ref):
    sums = jnp.sum(sums_ref[...], axis=0)
    alpha_ref[...] = sums[0:1] / sums[1:2]


def quotient(sums):
    return pl.pallas_call(
        quotient_kernel,
        out_shape=shape(1, sums.shape[2], F32),
        in_specs=[whole()],
        out_specs=whole(),
        compiler_params=params(8),
        name="quotient",
    )(sums)


def update_kernel(sizes, alpha_ref, right_ref, *refs):
    count = len(sizes)
    dirs, qs = refs[:count], refs[count : 2 * count]
    solution_ref, residual_ref, solution_buf, residual_buf, sems = refs[2 * count :]
    copies = []
    for i, (begin, size) in enumerate(zip(starts(sizes), sizes)):
        cols = slice(begin, begin + size)
        alpha = alpha_ref[:, cols]
        solution_buf[:, cols] = alpha * dirs[i][...].astype(F32)
        residual_buf[:, cols] = right_ref[:, cols] - alpha * qs[i][...]
        for k, (buf, ref) in enumerate(
            ((solution_buf, solution_ref), (residual_buf, residual_ref))
        ):
            copy = pltpu.make_async_copy(buf.at[:, cols], ref.at[:, cols], sems.at[2 * i + k])
            copy.start()
            copies.append(copy)
    for copy in copies:
        copy.wait()


def update(alpha, right_side, dirs, qs, sizes):
    rows, columns = right_side.shape
    out = shape(rows, columns, F32)
    return pl.pallas_call(
        functools.partial(update_kernel, sizes),
        out_shape=[out, out],
        in_specs=[whole()] * (2 + 2 * len(sizes)),
        out_specs=[whole(pl.ANY)] * 2,
        scratch_shapes=[pltpu.VMEM((rows, columns), F32)] * 2
        + [pltpu.SemaphoreType.DMA((2 * len(sizes),))],
        compiler_params=params(12),
        name="update",
    )(alpha, right_side, *dirs, *qs)


def body(right_side, schur, inv_factor, coarse_inverse, primal_index, phase, phase_coef):
    face_rows, columns = right_side.shape
    sizes = widths(columns)
    begins = starts(sizes)
    chunks = range(len(sizes))
    subs, groups = lax.axis_size("sub"), lax.axis_size("grp")
    rank = primal_index.shape[1]
    position, group = lax.axis_index("sub"), lax.axis_index("grp")
    place = jnp.stack([position % 2, group % 2, position]).astype(jnp.int32)
    place = lax.optimization_barrier(place)

    known = {}

    def get(name):
        if name not in known:
            known[name] = None
            known[name] = made[name[0]](*([int(name[1:])] if name[1:] else []))
        assert known[name] is not None
        return known[name]

    def tied(name, value):
        others = [get(other) for other in TIES.get(name, ())]
        return after(value, *others) if others else value

    primal_index = pltpu.with_memory_space_constraint(primal_index, pltpu.HBM)
    in_hbm = pltpu.with_memory_space_constraint(right_side, pltpu.HBM)
    first = first_chunk(place, in_hbm, sizes[0])
    own_primal = pick(in_hbm, primal_index, first)
    resid = split(right_side, first, sizes)

    masks = range(0, subs, 2)
    def gather(i):
        return exchange(tied(f"a{i}", own_primal), "sub", masks[i])

    def solved():
        pieces = [tied("e", own_primal)] + [get(f"a{i}") for i in range(1, len(masks))]
        return solve(place, coarse_inverse, pieces, masks)

    def coarse():
        own, partner = get("e")
        return own + pair_swap(tied("c", partner))

    def total():
        value = tied("t", get("c"))
        for step in powers(0, groups):
            value = value + exchange(value, "grp", step)
            if step == 1:
                value = tied("u", value)
        return get("c") + value / groups

    def direction(i):
        own = tied(f"d{i}", resid[i])
        if i:
            own = after(own, get(f"d{i - 1}")[0])
        return direction_chunk(
            place, primal_index, get("g")[1], get("m"), get(f"s{i}"), own, get(f"p{i}"), right_side,
            get("h"), begins[i],
        )

    def coefficients():
        labels = jnp.arange(phase_coef.shape[0], dtype=jnp.int32)
        coef = jnp.sum(
            jnp.where(phase[:, None] == labels[None, :], phase_coef[None, :], 0.0), axis=1
        )
        return jnp.broadcast_to(coef[:, None], (face_rows, 128))

    def image(i):
        own = tied(f"i{i}", get(f"d{i}")[0])
        if i:
            own = after(own, get(f"i{i - 1}")[1])
        return image_chunk(
            place, schur, get("n"), get(f"x{i}"), own, get(f"y{i}"), get("k")
        )

    made = {
        "a": gather,
        "s": lambda i: pair_swap(tied(f"s{i}", resid[i])),
        "p": lambda i: pass_on(tied(f"p{i}", get(f"s{i}"))),
        "g": lambda: gram(tied("g", inv_factor)),
        "m": lambda: to_left(get("g")[0]),
        "n": lambda: to_left(tied("n", schur)[:face_rows]),
        "e": solved,
        "c": coarse,
        "h": lambda: tied("h", total()),
        "d": direction,
        "x": lambda i: pair_swap(tied(f"x{i}", get(f"d{i}")[0])),
        "y": lambda i: pass_on(tied(f"y{i}", get(f"x{i}"))),
        "k": coefficients,
        "i": image,
    }
    images = [get(f"i{i}") for i in chunks]
    dirs = [get(f"d{i}") for i in chunks]
    alpha = step_length([d[1] for d in dirs], [i[1] for i in images], place[1] == 1)
    return update(alpha, right_side, [d[0] for d in dirs], [i[0] for i in images], sizes)


def solution(mesh):
    in_specs = (
        P(("grp", "sub"), None),
        P(("grp", "sub"), None),
        P(("grp", "sub"), None),
        P("grp", None),
        P(("grp", "sub"), None),
        P(("grp", "sub")),
        P(),
    )
    out_specs = (P(("grp", "sub"), None), P(("grp", "sub"), None))
    return jax.shard_map(body, mesh=mesh, in_specs=in_specs, out_specs=out_specs, check_vma=False)
```

```python
import functools

import jax
import jax.numpy as jnp
from jax import lax
from jax.experimental import pallas as pl
from jax.experimental.pallas import tpu as pltpu
from jax.sharding import PartitionSpec as P

HIGHEST = lax.Precision.HIGHEST
VMEM = pltpu.VMEM
SMEM = pltpu.SMEM
F32 = jnp.float32
BF16 = jnp.bfloat16

EIGHTHS = (2, 2, 2, 2)
TIES = {
    "d0": ("p1", "s2"),
    "d3": ("n", "x0"),
    "e": ("s0",),
    "g": ("c", "e"),
    "h": ("m", "s1"),
    "i0": ("x1",),
    "i1": ("x2",),
    "i2": ("x3",),
    "n": ("s2",),
    "p2": ("p0",),
    "p3": ("p2",),
    "s1": ("s0",),
    "s2": ("c", "s0"),
    "s3": ("m",),
    "t": ("s1",),
    "u": ("p0",),
}


def widths(columns):
    return [columns // 8 * part for part in EIGHTHS]


def starts(sizes):
    return [sum(sizes[:i]) for i in range(len(sizes))]


def params(mebibytes):
    return pltpu.CompilerParams(vmem_limit_bytes=mebibytes * 1024 * 1024)


def whole(space=VMEM):
    return pl.BlockSpec(memory_space=space)


def shape(rows, columns, dtype):
    return jax.ShapeDtypeStruct((rows, columns), dtype)


def after(value, *others):
    return lax.optimization_barrier((value,) + others)[0]


def exchange(value, axis, step):
    count = lax.axis_size(axis)
    return lax.ppermute(value, axis, [(i, i ^ step) for i in range(count)])


def pair_swap(value):
    return exchange(value, "sub", 1)


def pass_on(value):
    count = lax.axis_size("sub")
    pairs = [(j, (j + (2 if j % 2 == 0 else -2)) % count) for j in range(count)]
    return lax.ppermute(value, "sub", pairs)


def to_left(value):
    count = lax.axis_size("sub")
    return lax.ppermute(value, "sub", [(j, (j - 1) % count) for j in range(count)])


def powers(low, count):
    return [1 << b for b in range(low, count.bit_length() - 1)]


def step_length(rzs, pqs, odd):
    groups, subs = lax.axis_size("grp"), lax.axis_size("sub")
    parts = jnp.concatenate([jnp.concatenate(p, axis=1) for p in (rzs, pqs)], axis=0)
    half = parts.shape[1] // 2
    low, high = parts[:, :half], parts[:, half:]
    mine = jnp.where(odd, high, low) + exchange(jnp.where(odd, low, high), "grp", 1)
    same = [[g * subs + j for g in range(p, groups, 2) for j in range(subs)] for p in range(2)]
    copies = jnp.broadcast_to(mine[None], (len(same[0]),) + mine.shape)
    sums = lax.all_to_all(copies, ("grp", "sub"), 0, 0, axis_index_groups=same, tiled=True)
    alpha = quotient(sums)
    other = exchange(alpha, "grp", 1)
    return jnp.concatenate([jnp.where(odd, other, alpha), jnp.where(odd, alpha, other)], axis=1)


def first_kernel(place_ref, right_ref, chunk_ref):
    chunk_ref[...] = right_ref[...].astype(BF16)


def first_chunk(place, right_side, size):
    rows = right_side.shape[0]
    block = pl.BlockSpec((rows, size), lambda i: (0, 0))
    return pl.pallas_call(
        first_kernel,
        grid=(1,),
        out_shape=shape(rows, size, BF16),
        in_specs=[whole(SMEM), block],
        out_specs=block,
        compiler_params=params(8),
        name="first",
    )(place, right_side)


def pick_kernel(index_ref, right_ref, after_ref, primal_ref, blocks, sems):
    rank = primal_ref.shape[0]
    copies = []
    for k in range(rank):
        begin = pl.multiple_of((index_ref[0, k] >> 3) << 3, 8)
        source = right_ref.at[pl.ds(begin, 8), :]
        copies.append(pltpu.make_async_copy(source, blocks.at[k], sems.at[k]))
        copies[-1].start()
    for k in range(rank):
        copies[k].wait()
        primal_ref[k : k + 1, :] = blocks[k, pl.ds(index_ref[0, k] & 7, 1), :]


def pick(right_side, primal_index, first):
    columns = right_side.shape[1]
    rank = primal_index.shape[1]
    return pl.pallas_call(
        pick_kernel,
        out_shape=shape(rank, columns, F32),
        in_specs=[whole(SMEM), whole(pl.ANY), whole(pl.ANY)],
        out_specs=whole(),
        scratch_shapes=[
            pltpu.VMEM((rank, 8, columns), F32),
            pltpu.SemaphoreType.DMA((rank,)),
        ],
        compiler_params=params(8),
        name="pick",
    )(primal_index, right_side, first)


def split_kernel(sizes, right_ref, after_ref, *chunk_refs):
    for begin, size, chunk_ref in zip(starts(sizes)[1:], sizes[1:], chunk_refs):
        chunk_ref[...] = right_ref[:, begin : begin + size].astype(BF16)


def split(right_side, first, sizes):
    rows = right_side.shape[0]
    outs = [shape(rows, size, BF16) for size in sizes[1:]]
    out = pl.pallas_call(
        functools.partial(split_kernel, sizes),
        out_shape=outs,
        in_specs=[whole(), whole(pl.ANY)],
        out_specs=[whole()] * len(outs),
        compiler_params=params(8),
        name="split",
    )(right_side, first)
    return [first] + list(out)


def gram_kernel(factor_ref, upper_ref, lower_ref):
    half = upper_ref.shape[0]
    dims = (((0,), (0,)), ((), ()))
    factor = factor_ref[...]
    product = lax.dot_general(factor, factor, dims, preferred_element_type=F32)
    upper_ref[...] = product[:half].astype(BF16)
    lower_ref[...] = product[half:].astype(BF16)


def gram(factor):
    size = factor.shape[0]
    out = shape(size // 2, size, BF16)
    return pl.pallas_call(
        gram_kernel,
        out_shape=[out, out],
        in_specs=[whole()],
        out_specs=[whole(), whole()],
        compiler_params=params(8),
        name="gram",
    )(factor)


def solve_kernel(masks, place_ref, matrix_ref, *refs):
    pieces, (own_ref, partner_ref, sorted_ref, rows_ref) = refs[: len(masks)], refs[len(masks) :]
    rank = own_ref.shape[0]
    position = place_ref[2]
    sorted_ref[...] = jnp.zeros_like(sorted_ref)
    for mask, piece in zip(masks, pieces):
        begin = pl.multiple_of((position ^ mask) * rank, rank)
        sorted_ref[pl.ds(begin, rank), :] = piece[...]
    for k, target in enumerate((position, position ^ 1)):
        rows = pl.ds(pl.multiple_of(target * rank, rank), rank)
        rows_ref[k * rank : (k + 1) * rank, :] = matrix_ref[rows, :]
    both = jnp.dot(
        rows_ref[...], sorted_ref[...], precision=HIGHEST, preferred_element_type=F32
    )
    own_ref[...] = both[:rank]
    partner_ref[...] = both[rank:]


def solve(place, matrix, pieces, masks):
    rank, columns = pieces[0].shape
    out = shape(rank, columns, F32)
    return pl.pallas_call(
        functools.partial(solve_kernel, masks),
        out_shape=[out, out],
        in_specs=[whole(SMEM)] + [whole()] * (1 + len(pieces)),
        out_specs=[whole(), whole()],
        scratch_shapes=[
            pltpu.VMEM((matrix.shape[1], columns), F32),
            pltpu.VMEM((2 * rank, matrix.shape[1]), F32),
        ],
        compiler_params=params(8),
        name="solve",
    )(place, matrix, *pieces)


def stencil(parity, low, up, swapped, own, passed):
    half = low.shape[0]
    even = parity == 0
    for_swapped = jnp.where(even, up[:, half:], low[:, :half])
    for_passed = jnp.where(even, low[:, :half], up[:, half:])
    dot = functools.partial(jnp.dot, preferred_element_type=F32)
    total = dot(low[:, half:], own) + dot(up[:, :half], own)
    total = total + dot(for_swapped, swapped)
    return total + dot(for_passed, passed)


def direction_kernel(
    cols, place_ref, index_ref, low_ref, up_ref, swapped_ref, own_ref, passed_ref, right_ref,
    corr_ref, dir_ref, rz_ref, full_ref,
):
    full_ref[...] = 0.5 * stencil(
        place_ref[0], low_ref[...], up_ref[...], swapped_ref[...], own_ref[...], passed_ref[...]
    )
    for k in range(corr_ref.shape[0]):
        row = pl.ds(index_ref[0, k], 1)
        full_ref[row, :] = full_ref[row, :] + corr_ref[k : k + 1, cols]
    full = full_ref[...]
    dir_ref[...] = full.astype(BF16)
    rz_ref[...] = jnp.sum(right_ref[:, cols] * full, axis=0, keepdims=True)


def direction_chunk(place, index, low, up, swapped, own, passed, right_side, corr, begin):
    rows, size = own.shape
    return pl.pallas_call(
        functools.partial(direction_kernel, slice(begin, begin + size)),
        out_shape=[shape(rows, size, BF16), shape(1, size, F32)],
        in_specs=[whole(SMEM)] * 2 + [whole()] * 7,
        out_specs=[whole(), whole()],
        scratch_shapes=[pltpu.VMEM((rows, size), F32)],
        compiler_params=params(12),
        name="direction",
    )(place, index, low, up, swapped, own, passed, right_side, corr)


def image_kernel(
    place_ref, panel_ref, up_ref, swapped_ref, own_ref, passed_ref, coef_ref, q_ref, pq_ref
):
    own = own_ref[...]
    half = own.shape[0]
    total = stencil(
        place_ref[0], panel_ref[half:, :], up_ref[...], swapped_ref[...], own, passed_ref[...]
    )
    own_f = own.astype(F32)
    q = total + coef_ref[:, :1] * own_f
    q_ref[...] = q
    pq_ref[...] = jnp.sum(own_f * q, axis=0, keepdims=True)


def image_chunk(place, schur, up, swapped, own, passed, coef):
    rows, size = own.shape
    return pl.pallas_call(
        image_kernel,
        out_shape=[pltpu.VMEM((rows, size), F32), shape(1, size, F32)],
        in_specs=[whole(SMEM)] + [whole()] * 6,
        out_specs=[whole(), whole()],
        compiler_params=params(12),
        name="image",
    )(place, schur, up, swapped, own, passed, coef)


def quotient_kernel(sums_ref, alpha_ref):
    sums = jnp.sum(sums_ref[...], axis=0)
    alpha_ref[...] = sums[0:1] / sums[1:2]


def quotient(sums):
    return pl.pallas_call(
        quotient_kernel,
        out_shape=shape(1, sums.shape[2], F32),
        in_specs=[whole()],
        out_specs=whole(),
        compiler_params=params(8),
        name="quotient",
    )(sums)


def update_kernel(sizes, alpha_ref, right_ref, *refs):
    count = len(sizes)
    dirs, qs = refs[:count], refs[count : 2 * count]
    solution_ref, residual_ref, solution_buf, residual_buf, sems = refs[2 * count :]
    copies = []
    for i, (begin, size) in enumerate(zip(starts(sizes), sizes)):
        cols = slice(begin, begin + size)
        alpha = alpha_ref[:, cols]
        solution_buf[:, cols] = alpha * dirs[i][...].astype(F32)
        residual_buf[:, cols] = right_ref[:, cols] - alpha * qs[i][...]
        for k, (buf, ref) in enumerate(
            ((solution_buf, solution_ref), (residual_buf, residual_ref))
        ):
            copy = pltpu.make_async_copy(buf.at[:, cols], ref.at[:, cols], sems.at[2 * i + k])
            copy.start()
            copies.append(copy)
    for copy in copies:
        copy.wait()


def update(alpha, right_side, dirs, qs, sizes):
    rows, columns = right_side.shape
    out = shape(rows, columns, F32)
    return pl.pallas_call(
        functools.partial(update_kernel, sizes),
        out_shape=[out, out],
        in_specs=[whole()] * (2 + 2 * len(sizes)),
        out_specs=[whole(pl.ANY)] * 2,
        scratch_shapes=[pltpu.VMEM((rows, columns), F32)] * 2
        + [pltpu.SemaphoreType.DMA((2 * len(sizes),))],
        compiler_params=params(12),
        name="update",
    )(alpha, right_side, *dirs, *qs)


def body(right_side, schur, inv_factor, coarse_inverse, primal_index, phase, phase_coef):
    face_rows, columns = right_side.shape
    sizes = widths(columns)
    begins = starts(sizes)
    chunks = range(len(sizes))
    subs, groups = lax.axis_size("sub"), lax.axis_size("grp")
    rank = primal_index.shape[1]
    position, group = lax.axis_index("sub"), lax.axis_index("grp")
    place = jnp.stack([position % 2, group % 2, position]).astype(jnp.int32)
    place = lax.optimization_barrier(place)

    known = {}

    def get(name):
        if name not in known:
            known[name] = None
            known[name] = made[name[0]](*([int(name[1:])] if name[1:] else []))
        assert known[name] is not None
        return known[name]

    def tied(name, value):
        others = [get(other) for other in TIES.get(name, ())]
        return after(value, *others) if others else value

    primal_index = pltpu.with_memory_space_constraint(primal_index, pltpu.HBM)
    in_hbm = pltpu.with_memory_space_constraint(right_side, pltpu.HBM)
    first = first_chunk(place, in_hbm, sizes[0])
    own_primal = pick(in_hbm, primal_index, first)
    resid = split(right_side, first, sizes)

    masks = range(0, subs, 2)
    def gather(i):
        return exchange(tied(f"a{i}", own_primal), "sub", masks[i])

    def solved():
        pieces = [tied("e", own_primal)] + [get(f"a{i}") for i in range(1, len(masks))]
        return solve(place, coarse_inverse, pieces, masks)

    def coarse():
        own, partner = get("e")
        return own + pair_swap(tied("c", partner))

    def total():
        value = tied("t", get("c"))
        for step in powers(0, groups):
            value = value + exchange(value, "grp", step)
            if step == 1:
                value = tied("u", value)
        return get("c") + value / groups

    def direction(i):
        own = tied(f"d{i}", resid[i])
        if i:
            own = after(own, get(f"d{i - 1}")[0])
        return direction_chunk(
            place, primal_index, get("g")[1], get("m"), get(f"s{i}"), own, get(f"p{i}"), right_side,
            get("h"), begins[i],
        )

    def coefficients():
        labels = jnp.arange(phase_coef.shape[0], dtype=jnp.int32)
        coef = jnp.sum(
            jnp.where(phase[:, None] == labels[None, :], phase_coef[None, :], 0.0), axis=1
        )
        return jnp.broadcast_to(coef[:, None], (face_rows, 128))

    def image(i):
        own = tied(f"i{i}", get(f"d{i}")[0])
        if i:
            own = after(own, get(f"i{i - 1}")[1])
        return image_chunk(
            place, schur, get("n"), get(f"x{i}"), own, get(f"y{i}"), get("k")
        )

    made = {
        "a": gather,
        "s": lambda i: pair_swap(tied(f"s{i}", resid[i])),
        "p": lambda i: pass_on(tied(f"p{i}", get(f"s{i}"))),
        "g": lambda: gram(tied("g", inv_factor)),
        "m": lambda: to_left(get("g")[0]),
        "n": lambda: to_left(tied("n", schur)[:face_rows]),
        "e": solved,
        "c": coarse,
        "h": lambda: tied("h", total()),
        "d": direction,
        "x": lambda i: pair_swap(tied(f"x{i}", get(f"d{i}")[0])),
        "y": lambda i: pass_on(tied(f"y{i}", get(f"x{i}"))),
        "k": coefficients,
        "i": image,
    }
    images = [get(f"i{i}") for i in chunks]
    dirs = [get(f"d{i}") for i in chunks]
    alpha = step_length([d[1] for d in dirs], [i[1] for i in images], place[1] == 1)
    return update(alpha, right_side, [d[0] for d in dirs], [i[0] for i in images], sizes)


def solution(mesh):
    in_specs = (
        P(("grp", "sub"), None),
        P(("grp", "sub"), None),
        P(("grp", "sub"), None),
        P("grp", None),
        P(("grp", "sub"), None),
        P(("grp", "sub")),
        P(),
    )
    out_specs = (P(("grp", "sub"), None), P(("grp", "sub"), None))
    return jax.shard_map(body, mesh=mesh, in_specs=in_specs, out_specs=out_specs, check_vma=False)
```

```python
import functools

import jax
import jax.numpy as jnp
from jax import lax
from jax.experimental import pallas as pl
from jax.experimental.pallas import tpu as pltpu
from jax.sharding import PartitionSpec as P

HIGHEST = lax.Precision.HIGHEST
VMEM = pltpu.VMEM
SMEM = pltpu.SMEM
F32 = jnp.float32
BF16 = jnp.bfloat16

EIGHTHS = (2, 2, 2, 2)
TIES = {
    "d0": ("p1", "s2"),
    "d3": ("n", "x0"),
    "e": ("s0",),
    "g": ("c", "e"),
    "h": ("m", "s1"),
    "i0": ("x1",),
    "i1": ("x2",),
    "i2": ("x3",),
    "n": ("s2",),
    "p2": ("p0",),
    "p3": ("p2",),
    "s1": ("s0",),
    "s2": ("c", "s0"),
    "s3": ("m",),
    "t": ("s1",),
    "u": ("p0",),
}


def widths(columns):
    return [columns // 8 * part for part in EIGHTHS]


def starts(sizes):
    return [sum(sizes[:i]) for i in range(len(sizes))]


def params(mebibytes):
    return pltpu.CompilerParams(vmem_limit_bytes=mebibytes * 1024 * 1024)


def whole(space=VMEM):
    return pl.BlockSpec(memory_space=space)


def shape(rows, columns, dtype):
    return jax.ShapeDtypeStruct((rows, columns), dtype)


def after(value, *others):
    return lax.optimization_barrier((value,) + others)[0]


def exchange(value, axis, step):
    count = lax.axis_size(axis)
    return lax.ppermute(value, axis, [(i, i ^ step) for i in range(count)])


def pair_swap(value):
    return exchange(value, "sub", 1)


def pass_on(value):
    count = lax.axis_size("sub")
    pairs = [(j, (j + (2 if j % 2 == 0 else -2)) % count) for j in range(count)]
    return lax.ppermute(value, "sub", pairs)


def to_left(value):
    count = lax.axis_size("sub")
    return lax.ppermute(value, "sub", [(j, (j - 1) % count) for j in range(count)])


def powers(low, count):
    return [1 << b for b in range(low, count.bit_length() - 1)]


def step_length(rzs, pqs, odd):
    groups, subs = lax.axis_size("grp"), lax.axis_size("sub")
    parts = jnp.concatenate([jnp.concatenate(p, axis=1) for p in (rzs, pqs)], axis=0)
    half = parts.shape[1] // 2
    low, high = parts[:, :half], parts[:, half:]
    mine = jnp.where(odd, high, low) + exchange(jnp.where(odd, low, high), "grp", 1)
    same = [[g * subs + j for g in range(p, groups, 2) for j in range(subs)] for p in range(2)]
    copies = jnp.broadcast_to(mine[None], (len(same[0]),) + mine.shape)
    sums = lax.all_to_all(copies, ("grp", "sub"), 0, 0, axis_index_groups=same, tiled=True)
    alpha = quotient(sums)
    other = exchange(alpha, "grp", 1)
    return jnp.concatenate([jnp.where(odd, other, alpha), jnp.where(odd, alpha, other)], axis=1)


def first_kernel(place_ref, right_ref, chunk_ref):
    chunk_ref[...] = right_ref[...].astype(BF16)


def first_chunk(place, right_side, size):
    rows = right_side.shape[0]
    block = pl.BlockSpec((rows, size), lambda i: (0, 0))
    return pl.pallas_call(
        first_kernel,
        grid=(1,),
        out_shape=shape(rows, size, BF16),
        in_specs=[whole(SMEM), block],
        out_specs=block,
        compiler_params=params(8),
        name="first",
    )(place, right_side)


def pick_kernel(index_ref, right_ref, after_ref, primal_ref, sems):
    copies = []
    for k in range(primal_ref.shape[0]):
        source = right_ref.at[pl.ds(index_ref[0, k], 1), :]
        copies.append(pltpu.make_async_copy(source, primal_ref.at[k : k + 1, :], sems.at[k]))
        copies[-1].start()
    for copy in copies:
        copy.wait()


def pick(right_side, primal_index, first):
    columns = right_side.shape[1]
    rank = primal_index.shape[1]
    return pl.pallas_call(
        pick_kernel,
        out_shape=shape(rank, columns, F32),
        in_specs=[whole(SMEM), whole(pl.ANY), whole(pl.ANY)],
        out_specs=whole(),
        scratch_shapes=[pltpu.SemaphoreType.DMA((rank,))],
        compiler_params=params(8),
        name="pick",
    )(primal_index, right_side, first)


def split_kernel(sizes, right_ref, after_ref, *chunk_refs):
    for begin, size, chunk_ref in zip(starts(sizes)[1:], sizes[1:], chunk_refs):
        chunk_ref[...] = right_ref[:, begin : begin + size].astype(BF16)


def split(right_side, first, sizes):
    rows = right_side.shape[0]
    outs = [shape(rows, size, BF16) for size in sizes[1:]]
    out = pl.pallas_call(
        functools.partial(split_kernel, sizes),
        out_shape=outs,
        in_specs=[whole(), whole(pl.ANY)],
        out_specs=[whole()] * len(outs),
        compiler_params=params(8),
        name="split",
    )(right_side, first)
    return [first] + list(out)


def gram_kernel(factor_ref, upper_ref, lower_ref):
    half = upper_ref.shape[0]
    dims = (((0,), (0,)), ((), ()))
    factor = factor_ref[...]
    product = lax.dot_general(factor, factor, dims, preferred_element_type=F32)
    upper_ref[...] = product[:half].astype(BF16)
    lower_ref[...] = product[half:].astype(BF16)


def gram(factor):
    size = factor.shape[0]
    out = shape(size // 2, size, BF16)
    return pl.pallas_call(
        gram_kernel,
        out_shape=[out, out],
        in_specs=[whole()],
        out_specs=[whole(), whole()],
        compiler_params=params(8),
        name="gram",
    )(factor)


def solve_kernel(masks, place_ref, matrix_ref, *refs):
    pieces, (own_ref, partner_ref, sorted_ref, rows_ref) = refs[: len(masks)], refs[len(masks) :]
    rank = own_ref.shape[0]
    position = place_ref[2]
    sorted_ref[...] = jnp.zeros_like(sorted_ref)
    for mask, piece in zip(masks, pieces):
        begin = pl.multiple_of((position ^ mask) * rank, rank)
        sorted_ref[pl.ds(begin, rank), :] = piece[...]
    for k, target in enumerate((position, position ^ 1)):
        rows = pl.ds(pl.multiple_of(target * rank, rank), rank)
        rows_ref[k * rank : (k + 1) * rank, :] = matrix_ref[rows, :]
    both = jnp.dot(
        rows_ref[...], sorted_ref[...], precision=HIGHEST, preferred_element_type=F32
    )
    own_ref[...] = both[:rank]
    partner_ref[...] = both[rank:]


def solve(place, matrix, pieces, masks):
    rank, columns = pieces[0].shape
    out = shape(rank, columns, F32)
    return pl.pallas_call(
        functools.partial(solve_kernel, masks),
        out_shape=[out, out],
        in_specs=[whole(SMEM)] + [whole()] * (1 + len(pieces)),
        out_specs=[whole(), whole()],
        scratch_shapes=[
            pltpu.VMEM((matrix.shape[1], columns), F32),
            pltpu.VMEM((2 * rank, matrix.shape[1]), F32),
        ],
        compiler_params=params(8),
        name="solve",
    )(place, matrix, *pieces)


def stencil(parity, low, up, swapped, own, passed):
    half = low.shape[0]
    even = parity == 0
    for_swapped = jnp.where(even, up[:, half:], low[:, :half])
    for_passed = jnp.where(even, low[:, :half], up[:, half:])
    dot = functools.partial(jnp.dot, preferred_element_type=F32)
    total = dot(low[:, half:], own) + dot(up[:, :half], own)
    total = total + dot(for_swapped, swapped)
    return total + dot(for_passed, passed)


def direction_kernel(
    cols, place_ref, index_ref, low_ref, up_ref, swapped_ref, own_ref, passed_ref, right_ref,
    corr_ref, dir_ref, rz_ref, full_ref,
):
    full_ref[...] = 0.5 * stencil(
        place_ref[0], low_ref[...], up_ref[...], swapped_ref[...], own_ref[...], passed_ref[...]
    )
    for k in range(corr_ref.shape[0]):
        row = pl.ds(index_ref[0, k], 1)
        full_ref[row, :] = full_ref[row, :] + corr_ref[k : k + 1, cols]
    full = full_ref[...]
    dir_ref[...] = full.astype(BF16)
    rz_ref[...] = jnp.sum(right_ref[:, cols] * full, axis=0, keepdims=True)


def direction_chunk(place, index, low, up, swapped, own, passed, right_side, corr, begin):
    rows, size = own.shape
    return pl.pallas_call(
        functools.partial(direction_kernel, slice(begin, begin + size)),
        out_shape=[shape(rows, size, BF16), shape(1, size, F32)],
        in_specs=[whole(SMEM)] * 2 + [whole()] * 7,
        out_specs=[whole(), whole()],
        scratch_shapes=[pltpu.VMEM((rows, size), F32)],
        compiler_params=params(12),
        name="direction",
    )(place, index, low, up, swapped, own, passed, right_side, corr)


def image_kernel(
    place_ref, panel_ref, up_ref, swapped_ref, own_ref, passed_ref, coef_ref, q_ref, pq_ref
):
    own = own_ref[...]
    half = own.shape[0]
    total = stencil(
        place_ref[0], panel_ref[half:, :], up_ref[...], swapped_ref[...], own, passed_ref[...]
    )
    own_f = own.astype(F32)
    q = total + coef_ref[:, :1] * own_f
    q_ref[...] = q
    pq_ref[...] = jnp.sum(own_f * q, axis=0, keepdims=True)


def image_chunk(place, schur, up, swapped, own, passed, coef):
    rows, size = own.shape
    return pl.pallas_call(
        image_kernel,
        out_shape=[pltpu.VMEM((rows, size), F32), shape(1, size, F32)],
        in_specs=[whole(SMEM)] + [whole()] * 6,
        out_specs=[whole(), whole()],
        compiler_params=params(12),
        name="image",
    )(place, schur, up, swapped, own, passed, coef)


def quotient_kernel(sums_ref, alpha_ref):
    sums = jnp.sum(sums_ref[...], axis=0)
    alpha_ref[...] = sums[0:1] / sums[1:2]


def quotient(sums):
    return pl.pallas_call(
        quotient_kernel,
        out_shape=shape(1, sums.shape[2], F32),
        in_specs=[whole()],
        out_specs=whole(),
        compiler_params=params(8),
        name="quotient",
    )(sums)


def update_kernel(sizes, alpha_ref, right_ref, *refs):
    count = len(sizes)
    dirs, qs = refs[:count], refs[count : 2 * count]
    solution_ref, residual_ref, solution_buf, residual_buf, sems = refs[2 * count :]
    copies = []
    for i, (begin, size) in enumerate(zip(starts(sizes), sizes)):
        cols = slice(begin, begin + size)
        alpha = alpha_ref[:, cols]
        solution_buf[:, cols] = alpha * dirs[i][...].astype(F32)
        residual_buf[:, cols] = right_ref[:, cols] - alpha * qs[i][...]
        for k, (buf, ref) in enumerate(
            ((solution_buf, solution_ref), (residual_buf, residual_ref))
        ):
            copy = pltpu.make_async_copy(buf.at[:, cols], ref.at[:, cols], sems.at[2 * i + k])
            copy.start()
            copies.append(copy)
    for copy in copies:
        copy.wait()


def update(alpha, right_side, dirs, qs, sizes):
    rows, columns = right_side.shape
    out = shape(rows, columns, F32)
    return pl.pallas_call(
        functools.partial(update_kernel, sizes),
        out_shape=[out, out],
        in_specs=[whole()] * (2 + 2 * len(sizes)),
        out_specs=[whole(pl.ANY)] * 2,
        scratch_shapes=[pltpu.VMEM((rows, columns), F32)] * 2
        + [pltpu.SemaphoreType.DMA((2 * len(sizes),))],
        compiler_params=params(12),
        name="update",
    )(alpha, right_side, *dirs, *qs)


def body(right_side, schur, inv_factor, coarse_inverse, primal_index, phase, phase_coef):
    face_rows, columns = right_side.shape
    sizes = widths(columns)
    begins = starts(sizes)
    chunks = range(len(sizes))
    subs, groups = lax.axis_size("sub"), lax.axis_size("grp")
    rank = primal_index.shape[1]
    position, group = lax.axis_index("sub"), lax.axis_index("grp")
    place = jnp.stack([position % 2, group % 2, position]).astype(jnp.int32)
    place = lax.optimization_barrier(place)

    known = {}

    def get(name):
        if name not in known:
            known[name] = None
            known[name] = made[name[0]](*([int(name[1:])] if name[1:] else []))
        assert known[name] is not None
        return known[name]

    def tied(name, value):
        others = [get(other) for other in TIES.get(name, ())]
        return after(value, *others) if others else value

    primal_index = pltpu.with_memory_space_constraint(primal_index, pltpu.HBM)
    in_hbm = pltpu.with_memory_space_constraint(right_side, pltpu.HBM)
    first = first_chunk(place, in_hbm, sizes[0])
    own_primal = pick(in_hbm, primal_index, first)
    resid = split(right_side, first, sizes)

    masks = range(0, subs, 2)
    def gather(i):
        return exchange(tied(f"a{i}", own_primal), "sub", masks[i])

    def solved():
        pieces = [tied("e", own_primal)] + [get(f"a{i}") for i in range(1, len(masks))]
        return solve(place, coarse_inverse, pieces, masks)

    def coarse():
        own, partner = get("e")
        return own + pair_swap(tied("c", partner))

    def total():
        value = tied("t", get("c"))
        for step in powers(0, groups):
            value = value + exchange(value, "grp", step)
            if step == 1:
                value = tied("u", value)
        return get("c") + value / groups

    def direction(i):
        own = tied(f"d{i}", resid[i])
        if i:
            own = after(own, get(f"d{i - 1}")[0])
        return direction_chunk(
            place, primal_index, get("g")[1], get("m"), get(f"s{i}"), own, get(f"p{i}"), right_side,
            get("h"), begins[i],
        )

    def coefficients():
        labels = jnp.arange(phase_coef.shape[0], dtype=jnp.int32)
        coef = jnp.sum(
            jnp.where(phase[:, None] == labels[None, :], phase_coef[None, :], 0.0), axis=1
        )
        return jnp.broadcast_to(coef[:, None], (face_rows, 128))

    def image(i):
        own = tied(f"i{i}", get(f"d{i}")[0])
        if i:
            own = after(own, get(f"i{i - 1}")[1])
        return image_chunk(
            place, schur, get("n"), get(f"x{i}"), own, get(f"y{i}"), get("k")
        )

    made = {
        "a": gather,
        "s": lambda i: pair_swap(tied(f"s{i}", resid[i])),
        "p": lambda i: pass_on(tied(f"p{i}", get(f"s{i}"))),
        "g": lambda: gram(tied("g", inv_factor)),
        "m": lambda: to_left(get("g")[0]),
        "n": lambda: to_left(tied("n", schur)[:face_rows]),
        "e": solved,
        "c": coarse,
        "h": lambda: tied("h", total()),
        "d": direction,
        "x": lambda i: pair_swap(tied(f"x{i}", get(f"d{i}")[0])),
        "y": lambda i: pass_on(tied(f"y{i}", get(f"x{i}"))),
        "k": coefficients,
        "i": image,
    }
    images = [get(f"i{i}") for i in chunks]
    dirs = [get(f"d{i}") for i in chunks]
    alpha = step_length([d[1] for d in dirs], [i[1] for i in images], place[1] == 1)
    return update(alpha, right_side, [d[0] for d in dirs], [i[0] for i in images], sizes)


def solution(mesh):
    in_specs = (
        P(("grp", "sub"), None),
        P(("grp", "sub"), None),
        P(("grp", "sub"), None),
        P("grp", None),
        P(("grp", "sub"), None),
        P(("grp", "sub")),
        P(),
    )
    out_specs = (P(("grp", "sub"), None), P(("grp", "sub"), None))
    return jax.shard_map(body, mesh=mesh, in_specs=in_specs, out_specs=out_specs, check_vma=False)
```
